32 devices in a mesh: groups: 2 (over x), gx: 8 (over z, y), gy: 2 (over core).
Axes of the slice: x: 2, y: 2, z: 4, core: 2. Of those that a mesh axis runs over, the one named last changes fastest.
Arguments:
- states: bfloat16 [384, 8192], P('groups', 'gx'), parts along dimension 0, may hold values from -6 to 6
- w_query: bfloat16 [8192, 8192], P('gx', 'gy'), may hold values from -0.0625 to 0.0625
- w_key_value: bfloat16 [8192, 2, 1024], P('gx', None, 'gy'), may hold values from -0.0625 to 0.0625
- w_out: bfloat16 [8192, 8192], P('gy', 'gx'), may hold values from -0.25 to 0.25
- cache_kv: bfloat16 [384, 2, 128, 1024], P(('groups', 'gx'), None, None, 'gy'), parts along dimension 0, may hold values from -140 to 140
- lengths: int32 [384], P(('groups', 'gx')), parts along dimension 0, may hold values from 1 to 128
- adapter_ids: int32 [384], P('groups'), parts along dimension 0, may hold values from 0 to 31, as said below
- placement: int32 [32], replicated, may hold values from 0 to 31, each once
- adapter_down: bfloat16 [32, 64, 8192], P('gx', None, 'gy'), may hold values from -0.25 to 0.25
- up_weight_slots: bfloat16 [32, 64, 8192], P(None, None, 'gx'), may hold values from -0.75 to 0.75
Outputs:
- output: bfloat16 [384, 8192], P(('groups', 'gy'), 'gx'), parts along dimension 0
The draws below stay inside these ranges and needn't reach their ends.
There are 2 independent parts, one for each index of `groups`. The reference program is written for one: setup_inputs(seed, part) draws one part's arguments, and reference() takes and returns one part's arrays. A program takes and returns all parts, laid end to end along the dimension named above; an argument that names none is the same for every part. Nothing has to cross between parts.
Inputs may be any that keep to these rules, and one draw needn't show every extreme that they name: `adapter_ids`: in every aligned block of 24 rows, one adapter, the same in all blocks of a part, is named by exactly 2 rows; every other adapter is named by at most one row of a block, and some other adapter by one row of every block. `placement`: each slot holds one adapter; slot s lies with index s // (32 / 8) of gx.
All inputs are finite; a program needn't handle non-finite values.
Results may differ from the reference program's by a relative error of at most 0.012.
The reference program's roundings to bfloat16 on the way (of `queries`, `new_key`, `new_value`, `old_weights`, `attended` and `lowrank`) count: a program that leaves them out, or rounds other values in their place, can miss the bound.
Values may be sent and summed in bfloat16 or wider, within the bound.
No kernel may reach another device: no remote copies, remote signals or barrier semaphores. Data moves between devices by JAX's collectives and lax.ppermute only.
A program may use at most 128 MiB of HBM per device.

```python
import math
import jax
import jax.numpy as jnp
from jax import lax

MODEL_WIDTH = 8192
HEADS = 64
KV_HEADS = 8
HEAD_DIM = 128
ADAPTER_RANK = 64
ADAPTER_COUNT = 32
ROWS_DEV = 24
SPAN = 128
ROWS = 192
HD = 8192
KVD = 1024


def draw_cache_kv(key, part):
    key = jax.random.fold_in(key, 11)
    value_key = jax.random.fold_in(key, 0)
    shape = (ROWS, 2, SPAN, KVD)
    values = jax.random.truncated_normal(value_key, -6.0, 6.0, shape, jnp.float32)
    return values.astype(jnp.bfloat16)


def draw_lengths(key, part):
    key = jax.random.fold_in(key, 12)
    value_key, chosen_key = jax.random.split(key)
    values = jax.random.randint(value_key, (ROWS,), 1, SPAN + 1)
    chosen = jax.random.randint(chosen_key, (), 0, ROWS)
    return jnp.where(jnp.arange(ROWS) == chosen, SPAN, values).astype(jnp.int32)


def draw_adapter_ids(key, part):
    key = jax.random.fold_in(key, 13)
    order_key, block_key = jax.random.split(key)
    shuffled = jax.random.permutation(order_key, ADAPTER_COUNT)
    hottest = shuffled[0]
    warm_id = shuffled[1]
    others = shuffled[2:]
    block_keys = jax.random.split(block_key, ROWS // ROWS_DEV)

    def one_block(single_key):
        pick_key, mix_key = jax.random.split(single_key)
        picked = jax.random.permutation(pick_key, ADAPTER_COUNT - 2)[:ROWS_DEV - 3]
        block_ids = jnp.concatenate([jnp.stack([hottest, hottest, warm_id]), others[picked]])
        return jax.random.permutation(mix_key, block_ids)
    return jax.vmap(one_block)(block_keys).reshape(ROWS).astype(jnp.int32)


def levels(stream_key, shape, cuts, smallest, largest):
    def one(axis_at, parts):
        draws = jax.random.uniform(jax.random.fold_in(jax.random.fold_in(stream_key, 6), axis_at), (parts,), jnp.float32, smallest / len(cuts), largest / len(cuts))
        return jnp.repeat(jnp.exp(draws), shape[axis_at] // parts).reshape((-1,) + (1,) * (len(shape) - axis_at - 1))

    factor_of = one(*cuts[0])
    for cut in cuts[1:]:
        factor_of = factor_of * one(*cut)
    return factor_of


def noise(key, shape, scale, limit, cuts=(), kind=jnp.bfloat16):
    loudness = levels(key, shape, cuts, -0.22, 0.18) if cuts else 1.0
    drawn = jax.random.normal(key, shape, jnp.float32) * scale * loudness
    return jnp.minimum(jnp.maximum(drawn, -limit), limit).astype(kind)


def setup_inputs(seed: int = 0, part: int = 0) -> dict:
    key_of = jax.random.split(jax.random.key(seed), 11)
    own_keys = jax.random.split(jax.random.fold_in(key_of[10], part), 11)
    return {
        "states": noise(own_keys[0], (ROWS, MODEL_WIDTH), 1.0, 6.0, ((1, 8),)),
        "w_query": noise(key_of[1], (MODEL_WIDTH, HD), MODEL_WIDTH ** -0.5, 0.0625, ((0, 8), (1, 2))),
        "w_key_value": noise(key_of[2], (MODEL_WIDTH, 2, KVD), MODEL_WIDTH ** -0.5, 0.0625, ((0, 8), (2, 2))),
        "w_out": noise(key_of[3], (HD, MODEL_WIDTH), (HD // 16) ** -0.5, 0.25, ((0, 2), (1, 8))),
        "cache_kv": draw_cache_kv(jax.random.fold_in(jax.random.fold_in(key_of[10], part), 71), part),
        "lengths": draw_lengths(jax.random.fold_in(jax.random.fold_in(key_of[10], part), 71), part),
        "adapter_ids": draw_adapter_ids(jax.random.fold_in(jax.random.fold_in(key_of[10], part), 71), part),
        "placement": jax.random.permutation(key_of[7], ADAPTER_COUNT).astype(jnp.int32),
        "adapter_down": noise(key_of[8], (ADAPTER_COUNT, ADAPTER_RANK, HD), (HD // 16) ** -0.5, 0.25, ((0, 8), (2, 2))),
        "up_weight_slots": noise(key_of[9], (ADAPTER_COUNT, ADAPTER_RANK, MODEL_WIDTH), ADAPTER_RANK ** -0.5, 0.75, ((2, 8),)),
    }


rope_base = 500000.0

def rotate(values, positions):
    half_dim = values.shape[-1] // 2
    frequency = jnp.exp(jnp.arange(half_dim, dtype=jnp.float32) * (-2.0 * math.log(rope_base) / values.shape[-1]))
    angles = positions.astype(jnp.float32)[:, None] * frequency[None, :]
    cosine = jnp.cos(angles)[:, None, :]
    sine_part = jnp.sin(angles)[:, None, :]
    lower_half = values[..., :half_dim]
    upper_half = values[..., half_dim:]
    return jnp.concatenate([lower_half * cosine - upper_half * sine_part, upper_half * cosine + lower_half * sine_part], axis=-1)

def attend(queries, new_key, new_value, cache, lengths):
    row_count = queries.shape[0]
    groups = new_key.shape[1]
    per_group = queries.shape[1] // groups
    head_dim = queries.shape[2]
    window = cache.shape[2]
    grouped = queries.reshape(row_count, groups, per_group, head_dim).astype(jnp.float32)
    cached_keys = cache[:, 0].reshape(row_count, window, groups, head_dim).astype(jnp.float32)
    cached_values = cache[:, 1].reshape(row_count, window, groups, head_dim).astype(jnp.float32)
    factor = 1.0 / math.sqrt(head_dim)
    scores = jnp.einsum('rgqd,rlgd->rgql', grouped, cached_keys) * factor
    visible = jnp.arange(window)[None, :] < lengths[:, None]
    scores = jnp.where(visible[:, None, None, :], scores, -1e+30)
    own_score = jnp.einsum('rgqd,rgd->rgq', grouped, new_key.astype(jnp.float32)) * factor
    highest = jnp.maximum(lax.optimization_barrier(jnp.max(scores, axis=-1)), own_score)
    old_terms = jnp.exp(scores - highest[..., None])
    newest = jnp.exp(own_score - highest)
    denominator = lax.optimization_barrier(jnp.sum(old_terms, axis=-1)) + newest
    old_weights = (old_terms / denominator[..., None]).astype(jnp.bfloat16)
    new_weight = (newest / denominator).astype(jnp.bfloat16)
    combined = jnp.einsum('rgql,rlgd->rgqd', old_weights.astype(jnp.float32), cached_values)
    combined = combined + new_weight.astype(jnp.float32)[..., None] * new_value.astype(jnp.float32)[:, :, None, :]
    return combined.reshape(row_count, groups * per_group * head_dim).astype(jnp.bfloat16)

def reference(states, w_query, w_key_value, w_out, cache_kv, lengths, adapter_ids, placement, adapter_down, up_weight_slots):
    projected_query = jnp.dot(states, w_query, preferred_element_type=jnp.float32)
    projected_pair = jnp.dot(states, w_key_value.reshape(MODEL_WIDTH, 2 * KVD), preferred_element_type=jnp.float32)
    projected_pair = projected_pair.reshape(ROWS, 2, KV_HEADS, HEAD_DIM)
    queries = rotate(projected_query.reshape(ROWS, HEADS, HEAD_DIM), lengths).astype(jnp.bfloat16)
    new_key = rotate(projected_pair[:, 0], lengths).astype(jnp.bfloat16)
    new_value = projected_pair[:, 1].astype(jnp.bfloat16)
    attended = attend(queries, new_key, new_value, cache_kv, lengths)
    slot_of = placement[adapter_ids].astype(jnp.int32)
    chosen = slot_of[:, None] == jnp.arange(ADAPTER_COUNT, dtype=jnp.int32)[None, :]
    shrunk = jnp.dot(attended, adapter_down.reshape(ADAPTER_COUNT * ADAPTER_RANK, HD).T, preferred_element_type=jnp.float32)
    shrunk = shrunk.reshape(ROWS, ADAPTER_COUNT, ADAPTER_RANK)
    lowrank = lax.optimization_barrier(jnp.sum(jnp.where(chosen[:, :, None], shrunk, jnp.zeros((), jnp.float32)), axis=1)).astype(jnp.bfloat16)
    spread_rows = jnp.where(chosen[:, :, None], lowrank[:, None, :], jnp.zeros((), jnp.bfloat16)).reshape(ROWS, ADAPTER_COUNT * ADAPTER_RANK)
    base_output = jnp.dot(attended, w_out, preferred_element_type=jnp.float32)
    adapter_update = jnp.dot(spread_rows, up_weight_slots.reshape(ADAPTER_COUNT * ADAPTER_RANK, MODEL_WIDTH), preferred_element_type=jnp.float32)
    return (base_output + adapter_update).astype(jnp.bfloat16)
```

```python
import functools
import math

import jax
import jax.numpy as jnp
from jax import lax
from jax.experimental import pallas as pl
from jax.experimental.pallas import tpu as pltpu
from jax.sharding import PartitionSpec as P

HEAD_DIM = 128
CHUNKS = 2
PIN = True
SPLIT = True
STAGE = False
STAGE_UP = False

rope_base = 500000.0


def rotation(positions):
    half_dim = HEAD_DIM // 2
    frequency = jnp.exp(
        jnp.arange(half_dim, dtype=jnp.float32) * (-2.0 * math.log(rope_base) / HEAD_DIM)
    )
    angles = positions.astype(jnp.float32)[:, None] * frequency[None, :]
    cosine, sine_part = jnp.cos(angles), jnp.sin(angles)
    return jnp.concatenate([cosine, cosine, -sine_part, sine_part], axis=1)


def split_copies(source, target, sems, pieces):
    count = source.shape[0] // pieces
    return [
        pltpu.make_async_copy(
            source.at[pl.ds(n * count, count)], target.at[pl.ds(n * count, count)], sems.at[n]
        )
        for n in range(pieces)
    ]


def stage_kernel(pieces, in_ref, out_ref, sems):
    copies = split_copies(in_ref, out_ref, sems, pieces)
    for copy in copies:
        copy.start()
    for copy in copies:
        copy.wait()


def stage(x):
    pieces = math.gcd(8, x.shape[0])
    return pl.pallas_call(
        functools.partial(stage_kernel, pieces),
        in_specs=[pl.BlockSpec(memory_space=pl.ANY)],
        out_specs=pl.BlockSpec(memory_space=pltpu.VMEM),
        out_shape=jax.ShapeDtypeStruct(x.shape, x.dtype),
        scratch_shapes=[pltpu.SemaphoreType.DMA((pieces,))],
        compiler_params=pltpu.CompilerParams(vmem_limit_bytes=24 * 2**20),
        cost_estimate=pl.CostEstimate(flops=0, bytes_accessed=2 * x.nbytes, transcendentals=0),
        name="stage",
    )(x)


def project_kernel(
    bit, local_rows, start, tile, side_ref, states_hbm, weight_hbm, away_ref, kept_ref,
    states_s, weight_s, sems,
):
    width, columns = weight_s.shape
    pieces = sems.shape[0] - 1
    depth = width // pieces
    copies = [pltpu.make_async_copy(states_hbm, states_s, sems.at[pieces])]
    for n in range(pieces):
        at = pl.ds(n * depth, depth)
        copies.append(
            pltpu.make_async_copy(
                weight_hbm.at[at, pl.ds(start, columns)], weight_s.at[at], sems.at[n]
            )
        )
    for copy in copies:
        copy.start()
    for copy in copies:
        copy.wait()
    even = side_ref[0] == 0
    for n in range(columns // tile):
        at = slice(n * tile, (n + 1) * tile)
        part = jnp.dot(states_s[...], weight_s[:, at], preferred_element_type=jnp.float32)
        sides = [
            jnp.concatenate(
                [
                    part[block * local_rows : (block + 1) * local_rows]
                    for block in range(part.shape[0] // local_rows)
                    if (block >> bit) % 2 == which
                ],
                axis=0,
            )
            for which in range(2)
        ]
        away_ref[:, at] = jnp.where(even, sides[1], sides[0]).astype(jnp.bfloat16)
        kept_ref[:, at] = jnp.where(even, sides[0], sides[1])


def project(side, states, weight, start, columns, bit, local_rows):
    rows, width = states.shape
    tile = math.gcd(512, columns)
    kept_rows = rows // 2
    pieces = math.gcd(8, width // 16)
    vmem = pl.BlockSpec(memory_space=pltpu.VMEM)
    hbm = pl.BlockSpec(memory_space=pl.ANY)
    return pl.pallas_call(
        functools.partial(project_kernel, bit, local_rows, start, tile),
        in_specs=[pl.BlockSpec(memory_space=pltpu.SMEM), hbm, hbm],
        out_specs=[vmem, vmem],
        out_shape=[
            jax.ShapeDtypeStruct((kept_rows, columns), jnp.bfloat16),
            jax.ShapeDtypeStruct((kept_rows, columns), jnp.float32),
        ],
        scratch_shapes=[
            pltpu.VMEM((rows, width), states.dtype),
            pltpu.VMEM((width, columns), weight.dtype),
            pltpu.SemaphoreType.DMA((pieces + 1,)),
        ],
        compiler_params=pltpu.CompilerParams(vmem_limit_bytes=58 * 2**20),
        cost_estimate=pl.CostEstimate(
            flops=2 * rows * width * columns,
            bytes_accessed=2 * width * (rows + columns) + 6 * kept_rows * columns,
            transcendentals=0,
        ),
        name="project",
    )(side, states, weight)


def attend_kernel(heads, groups, far, offsets, lengths_ref, trig_ref, *refs):
    q_refs = refs[: far + 1]
    kv_refs = refs[far + 1 : 2 * far + 2]
    cache_s, out_ref, q_s, k_s, v_s, o_s = refs[2 * far + 2 :]
    per_group = heads // groups
    q_start, key_start, value_start = offsets
    rows, _, window, columns = cache_s.shape

    cosine = trig_ref[:, :HEAD_DIM]
    signed = trig_ref[:, HEAD_DIM:]

    def total(parts, start):
        value = parts[0][:, start : start + HEAD_DIM]
        for ref in parts[1:]:
            value = value + ref[:, start : start + HEAD_DIM].astype(jnp.float32)
        return value

    def turned(value):
        value = value * cosine + pltpu.roll(value, HEAD_DIM // 2, 1) * signed
        return value.astype(jnp.bfloat16).astype(jnp.float32)

    q_s[...] = jnp.zeros_like(q_s)
    for g in range(groups):
        key = turned(total(kv_refs, key_start + g * HEAD_DIM))
        value = total(kv_refs, value_start + g * HEAD_DIM)
        value = value.astype(jnp.bfloat16).astype(jnp.float32)
        for j in range(g * per_group, (g + 1) * per_group):
            q_s[:, j, g * HEAD_DIM : (g + 1) * HEAD_DIM] = turned(
                total(q_refs, q_start + j * HEAD_DIM)
            )
            k_s[:, j, :] = key
            v_s[:, j, :] = value

    factor = 1.0 / math.sqrt(HEAD_DIM)
    slot = lax.broadcasted_iota(jnp.int32, (heads, window), 1)
    q = q_s[...]
    flat = q[:, :, :HEAD_DIM]
    for g in range(1, groups):
        flat = flat + q[:, :, g * HEAD_DIM : (g + 1) * HEAD_DIM]
    own = jnp.sum(flat * k_s[...], axis=2, keepdims=True) * factor
    low = q.astype(jnp.bfloat16)
    scores = []
    for r in range(rows):
        score = lax.dot_general(
            low[r],
            cache_s[r, 0],
            (((1,), (1,)), ((), ())),
            preferred_element_type=jnp.float32,
        )
        scores.append(jnp.where(slot < lengths_ref[r], score * factor, -1e30))
    scores = jnp.stack(scores, axis=0)
    highest = jnp.maximum(jnp.max(scores, axis=2, keepdims=True), own)
    old_terms = jnp.exp(scores - highest)
    newest = jnp.exp(own - highest)
    denominator = jnp.sum(old_terms, axis=2, keepdims=True) + newest
    old_weights = (old_terms / denominator).astype(jnp.bfloat16)
    new_weight = (newest / denominator).astype(jnp.bfloat16).astype(jnp.float32)
    added = new_weight * v_s[...]
    for r in range(rows):
        mixed = jnp.dot(old_weights[r], cache_s[r, 1], preferred_element_type=jnp.float32)
        mixed = jnp.concatenate(
            [
                mixed[g * per_group : (g + 1) * per_group, g * HEAD_DIM : (g + 1) * HEAD_DIM]
                for g in range(groups)
            ],
            axis=0,
        )
        o_s[r] = mixed + added[r]
    for j in range(heads):
        out_ref[:, j * HEAD_DIM : (j + 1) * HEAD_DIM] = o_s[:, j, :].astype(jnp.bfloat16)


def attend(chunk, heads, groups, offsets, lengths, trig, q_parts, kv_parts, cache):
    rows, _, window, _ = cache.shape

    def whole(x):
        return pl.BlockSpec(x.shape, lambda i, s: (0,) * x.ndim)

    far = len(q_parts) - 1
    small = [trig, *q_parts, *kv_parts]
    return pl.pallas_call(
        functools.partial(attend_kernel, heads, groups, far, offsets),
        grid_spec=pltpu.PrefetchScalarGridSpec(
            num_scalar_prefetch=1,
            grid=(1,),
            in_specs=[whole(x) for x in small]
            + [
                pl.BlockSpec(
                    (rows, 2, window, groups * HEAD_DIM), lambda i, s: (0, 0, 0, chunk)
                )
            ],
            out_specs=pl.BlockSpec((rows, heads * HEAD_DIM), lambda i, s: (0, 0)),
            scratch_shapes=[
                pltpu.VMEM((rows, heads, groups * HEAD_DIM), jnp.float32),
                pltpu.VMEM((rows, heads, HEAD_DIM), jnp.float32),
                pltpu.VMEM((rows, heads, HEAD_DIM), jnp.float32),
                pltpu.VMEM((rows, heads, HEAD_DIM), jnp.float32),
            ],
        ),
        out_shape=jax.ShapeDtypeStruct((rows, heads * HEAD_DIM), jnp.bfloat16),
        compiler_params=pltpu.CompilerParams(vmem_limit_bytes=24 * 2**20),
        cost_estimate=pl.CostEstimate(
            flops=4 * rows * heads * window * HEAD_DIM * groups,
            bytes_accessed=4 * rows * window * groups * HEAD_DIM,
            transcendentals=rows * heads * window,
        ),
        name="attend",
    )(lengths, *small, cache)


def finish_kernel(
    local_rows, place_ref, slots_ref, low_ref, kept_ref, sent_ref, up_ref, out_ref, placed
):
    rows, rank = low_ref.shape
    depth = up_ref.shape[0]
    wide = math.gcd(256, depth)
    blocks = rows // (2 * local_rows)
    for which in range(2):
        for line in range(blocks):
            start = (which * blocks + line) * local_rows
            at = slice(start, start + local_rows)
            target = 2 * (line ^ place_ref[1]) + (which ^ place_ref[0])
            target = pl.multiple_of(target * local_rows, 8)
            placed[pl.ds(target, local_rows), :] = kept_ref[at, :] + sent_ref[at, :]
    low = jnp.concatenate([low_ref[...].astype(jnp.float32)] * (wide // rank), axis=1)
    offset = slots_ref[...] - lax.broadcasted_iota(jnp.int32, (rows, wide), 1) // rank
    total = placed[...]
    for start in range(0, depth, wide):
        spread = jnp.where(offset == start // rank, low, 0.0).astype(jnp.bfloat16)
        total = total + jnp.dot(
            spread, up_ref[start : start + wide, :], preferred_element_type=jnp.float32
        )
    out_ref[...] = total.astype(jnp.bfloat16)


def finish(local_rows, place, slots, low_rank, kept, sent, up):
    rows, columns = kept.shape
    vmem = pl.BlockSpec(memory_space=pltpu.VMEM)
    return pl.pallas_call(
        functools.partial(finish_kernel, local_rows),
        in_specs=[pl.BlockSpec(memory_space=pltpu.SMEM)] + [vmem] * 5,
        out_specs=vmem,
        out_shape=jax.ShapeDtypeStruct((rows, columns), jnp.bfloat16),
        scratch_shapes=[pltpu.VMEM((rows, columns), jnp.float32)],
        compiler_params=pltpu.CompilerParams(vmem_limit_bytes=24 * 2**20),
        cost_estimate=pl.CostEstimate(
            flops=2 * rows * up.shape[0] * columns,
            bytes_accessed=2 * up.shape[0] * columns,
            transcendentals=0,
        ),
        name="finish",
    )(place, slots, low_rank, kept, sent, up)


def lookup_slots(row_ids, placement):
    adapters = placement.shape[0]
    matching = row_ids[:, None] == jnp.arange(adapters, dtype=jnp.int32)[None, :]
    return jnp.sum(jnp.where(matching, placement[None, :], 0), axis=1)


def on_device(
    states,
    w_query,
    w_key_value,
    w_out,
    cache_kv,
    lengths,
    adapter_ids,
    placement,
    adapter_down,
    up_weight_slots,
):
    owners = lax.axis_size("gx")
    lines = owners // 2
    local_rows = cache_kv.shape[0]
    side_rows = lines * local_rows
    half_rows = side_rows // 2
    me = lax.axis_index("gx")
    half = lax.axis_index("gy")
    my_line, my_side = me // 2, me % 2
    line_bits = [1 << n for n in range(lines.bit_length() - 1)]

    def my_bit(bit):
        return (my_line // bit) % 2

    def swap(x, bit):
        return lax.ppermute(x, "gx", [(i, i ^ bit) for i in range(owners)])

    def swap_half(x):
        return lax.ppermute(x, "gy", [(0, 1), (1, 0)])

    q_cols = w_query.shape[1] // CHUNKS
    kv_cols = w_key_value.shape[2]
    side = my_side.astype(jnp.int32).reshape(1)
    trig = rotation(lengths)
    pair = w_key_value.reshape(w_key_value.shape[0], 2 * kv_cols)

    bits = list(range(owners.bit_length() - 1))

    def bit_of(bit):
        return (me >> bit) % 2

    def projected(states, weight, start, columns, bit):
        mine = bit_of(bit).astype(jnp.int32).reshape(1)
        away, kept = project(mine, states, weight, start, columns, bit, local_rows)
        away, kept, states = lax.optimization_barrier((away, kept, states))
        return (kept, swap(away, 1 << bit)), states

    side_first, line_first = bits, bits[1:] + bits[:1]
    first, states = projected(states, w_query, 0, q_cols, side_first[0])
    second, states = projected(states, w_query, q_cols, q_cols, line_first[0])
    pairs, states = projected(states, pair, 0, 2 * kv_cols, side_first[0])
    sums = [first, second, pairs]
    orders = [side_first, line_first, side_first]
    left = [[bit for bit in bits if bit != order[0]] for order in orders]
    before = None
    for n, at in [(n, at) for at in range(1, len(bits)) for n in ((0, 1, 2) if at == 1 else (0, 2, 1))]:
        kept, got = sums[n]
        if before is not None:
            got, _ = lax.optimization_barrier((got, before))
        before = got
        bit, columns = orders[n][at], kept.shape[1]
        inner = (1 << left[n].index(bit)) * local_rows
        left[n].remove(bit)
        total = (kept + got.astype(jnp.float32)).reshape(-1, 2, inner, columns)
        away = lax.dynamic_index_in_dim(total, 1 - bit_of(bit), 1, keepdims=False)
        home = lax.dynamic_index_in_dim(total, bit_of(bit), 1, keepdims=False)
        away = away.reshape(-1, columns).astype(jnp.bfloat16)
        if PIN:
            before = (before, away)
        sums[n] = (home.reshape(-1, columns), swap(away, 1 << bit))
    q_sums, (kv_sums, kv_at) = sums[:2], (sums[2], 0)

    groups = kv_cols // HEAD_DIM // CHUNKS
    attended = []
    for c in range(CHUNKS):
        key_at = kv_at + c * groups * HEAD_DIM
        if c:
            far, _ = lax.optimization_barrier((q_sums[c][-1], attended[-1]))
            q_sums[c] = (*q_sums[c][:-1], far)
        attended.append(
            attend(
                c,
                q_cols // HEAD_DIM,
                groups,
                (0, key_at, key_at + kv_cols),
                lengths,
                trig,
                q_sums[c],
                kv_sums,
                cache_kv,
            )
        )

    local_slots = adapter_down.shape[0]
    rank = adapter_down.shape[1]
    down = adapter_down.reshape(local_slots * rank, adapter_down.shape[2])

    def product(x, weight, axis, c):
        at = c * q_cols
        return lax.dot_general(
            x[:, at : at + q_cols],
            lax.slice_in_dim(weight, at, at + q_cols, axis=axis),
            (((1,), (axis,)), ((), ())),
            preferred_element_type=jnp.float32,
        )

    def summed(x, weight, axis):
        return sum(product(x, weight, axis, c) for c in range(CHUNKS))

    own = jnp.concatenate(attended, axis=1)
    far = lines // 2
    blocks = [own, *(swap(own, 2 << n) for n in range(len(line_bits)))]
    blocks = {0: own, **{bit: x for bit, x in zip(line_bits, blocks[1:])}}
    crossing = [swap(own, 1)]
    for k in range(1, far):
        if k not in blocks:
            blocks[k] = swap(blocks[k & (k - 1)], 2 * (k & -k))
    early = jnp.concatenate([blocks[k] for k in range(far)] + crossing, axis=0)
    out_early, shrunk_early = summed(early, w_out, 0), summed(early, down, 1)
    blocks[far], out_early, shrunk_early = lax.optimization_barrier(
        (blocks[far], out_early, shrunk_early)
    )
    for k in range(far + 1, lines):
        blocks[k] = swap(blocks[k & (k - 1)], 2 * (k & -k))
    blocks = [blocks[k] for k in range(lines)]
    crossing += [swap(x, 1) for x in blocks[1:]]
    late = jnp.concatenate(blocks[far:] + crossing[1:], axis=0)
    shrunk_late = summed(late, down, 1)
    up = up_weight_slots.reshape(-1, up_weight_slots.shape[2])

    def by_side(early, late):
        return [
            jnp.concatenate([early[:half_rows], late[:half_rows]], axis=0),
            jnp.concatenate([early[half_rows:], late[half_rows:]], axis=0),
        ]

    shrunk = by_side(shrunk_early, shrunk_late)

    slots = lookup_slots(adapter_ids, placement)
    here = slots[:, None] == me * local_slots + jnp.arange(local_slots)[None, :]
    x = jnp.stack(shrunk, axis=0).reshape(
        (2, 2) + (2,) * (len(line_bits) - 1) + (local_rows, local_slots, rank)
    )
    places = [my_side] + [my_bit(bit) for bit in reversed(line_bits)]
    for axis, place in enumerate(places):
        x = jnp.where(place == 0, x, jnp.flip(x, axis))
    x = jnp.moveaxis(x, 0, len(line_bits)).reshape(-1, local_slots, rank)
    x = jnp.sum(jnp.where(here[:, :, None], x, jnp.zeros(())), axis=1)

    def part(x, which):
        return lax.dynamic_slice_in_dim(x, which * side_rows, side_rows, 0)

    low_rank = (part(x, half) + swap_half(part(x, 1 - half))).astype(jnp.bfloat16)
    turns = [late] * CHUNKS
    turns[0], low_rank = lax.optimization_barrier((late, low_rank))
    low_rank = low_rank + swap(low_rank, 1)
    if SPLIT:
        turns[-1], low_rank = lax.optimization_barrier((late, low_rank))
    else:
        turns[-1] = turns[0]
    for x in [swap(low_rank, 2 * k) for k in range(1, lines)]:
        low_rank = low_rank + x

    out_late = sum(
        lax.optimization_barrier(product(turns[c], w_out, 0, c)) for c in range(CHUNKS)
    )
    same = my_bit(line_bits[-1]) == half
    outs = by_side(out_early, out_late)
    halves = [(x[:half_rows], x[half_rows:]) for x in outs]
    home = jnp.concatenate([jnp.where(same, *x) for x in halves], axis=0)
    away = jnp.concatenate([jnp.where(same, *x[::-1]) for x in halves], axis=0)
    place = jnp.stack([my_side, my_line % max(lines // 2, 1)]).astype(jnp.int32)
    return finish(
        local_rows,
        place,
        part(slots, half)[:, None],
        low_rank,
        home,
        swap_half(away),
        up,
    )


def solution(mesh):
    return jax.shard_map(
        on_device,
        mesh=mesh,
        in_specs=(
            P("groups", "gx"),
            P("gx", "gy"),
            P("gx", None, "gy"),
            P("gy", "gx"),
            P(("groups", "gx"), None, None, "gy"),
            P(("groups", "gx")),
            P("groups"),
            P(),
            P("gx", None, "gy"),
            P(None, None, "gx"),
        ),
        out_specs=P(("groups", "gy"), "gx"),
        check_vma=False,
    )
```
